32 devices in a mesh: parts: 2 (over x), space: 16 (over z, y, core).
Axes of the slice: x: 2, y: 2, z: 4, core: 2. Of those that a mesh axis runs over, the one named last changes fastest.
Arguments:
- obs: bfloat16 [192, 256, 512], P(('parts', 'space')), parts along dimension 0, may hold values from -16 to 16
- counts: int32 [192], P(('parts', 'space')), parts along dimension 0, may hold values from 64 to 256, as said below
- neighbours: int32 [192, 4], P(('parts', 'space')), parts along dimension 0, may hold values from -1 to 94, as said below
- krig: bfloat16 [192, 4, 256, 256], P(('parts', 'space')), parts along dimension 0, may hold values from -0.1875 to 0.1875
- knot_load: bfloat16 [192, 256, 2048], P(('parts', 'space')), parts along dimension 0, may hold values from -0.1875 to 0.1875
- knot_values: bfloat16 [4096, 512], P(('parts', 'space')), parts along dimension 0, may hold values from -6 to 6
- whiten: bfloat16 [192, 256, 256], P(('parts', 'space')), parts along dimension 0, may hold values from -1 to 2, as said below
- noise_var: float32 [512], replicated, may hold values from 0.2 to 1
Outputs:
- posterior: bfloat16 [192, 256, 512], P(('parts', 'space')), parts along dimension 0
- average_loglik: float32 [1024], P('parts'), parts along dimension 0
- knot_score: float32 [4096, 512], P(('parts', 'space')), parts along dimension 0
The draws below stay inside these ranges and needn't reach their ends.
There are 2 independent parts, one for each index of `parts`. The reference program is written for one: setup_inputs(seed, part) draws one part's arguments, and reference() takes and returns one part's arrays. A program takes and returns all parts, laid end to end along the dimension named above; an argument that names none is the same for every part. Nothing has to cross between parts.
Inputs may be any that keep to these rules, and one draw needn't show every extreme that they name: `neighbours`: entry 0 of block b's list is b - 1 (-1 for block 0); the other entries are distinct ids from b - 9 to b - 2, or -1. A block's valid points are its first counts[b] points; the rest is padding. `whiten`: each block's factor is lower triangular with a positive diagonal.
All inputs are finite; a program needn't handle non-finite values.
Results may differ from the reference program's by a relative error of at most 0.00105.
The reference program's roundings to bfloat16 on the way (of `masked`, `near_rows`, `residual`, `whitened_half`, `adjoint_half` and `returned`) count: a program that leaves them out, or rounds other values in their place, can miss the bound.
Values may be sent and summed in bfloat16 or wider, within the bound.
A program may use at most 128 MiB of HBM per device.

```python
import math
import jax
import jax.numpy as jnp
from jax import lax

PTS = 256
KNOTS = 2048
NEIGH = 4
SLOTS = 6
FIELDS = 512
REACH = 9
NBLK = 96
N_SPACE = 16


def draw_obs(key, part):
    key = jax.random.fold_in(key, 7)
    key_base, key_column = jax.random.split(key, 2)
    rising = 1.0 + 2.0 * jnp.arange(NBLK, dtype=jnp.float32) / max(NBLK - 1, 1)
    column = jnp.exp(jax.random.uniform(key_column, (FIELDS,), minval=math.log(0.5), maxval=math.log(2.0)))
    values = jax.random.normal(key_base, (NBLK, PTS, FIELDS)) * rising[:, None, None] * column[None, None, :]
    return jnp.clip(values, -16.0, 16.0).astype(jnp.bfloat16)


def draw_counts(key, part):
    key = jax.random.fold_in(key, 13)
    key_base, key_low, key_gap = jax.random.split(key, 3)
    values = jax.random.randint(key_base, (NBLK,), PTS // 4, PTS + 1)
    low_index = jax.random.randint(key_low, (), 0, NBLK)
    high_index = (low_index + 1 + jax.random.randint(key_gap, (), 0, NBLK - 1)) % NBLK
    values = values.at[low_index].set(PTS // 4).at[high_index].set(PTS)
    return values.astype(jnp.int32)


def draw_neighbours(key, part):
    key = jax.random.fold_in(key, 11)
    key_order, key_keep = jax.random.split(key)
    span = REACH - 1
    scores = jax.random.randint(key_order, (NBLK, span), 0, 1 << 20) * span + jnp.arange(span, dtype=jnp.int32)[None, :]
    _, order = lax.top_k(scores, NEIGH - 1)
    offsets = order + 2
    keeping = jax.random.randint(key_keep, (NBLK, NEIGH - 1), 0, 5) > 0
    block_ids = jnp.arange(NBLK, dtype=jnp.int32)
    others = block_ids[:, None] - offsets
    others = jnp.where(keeping & (others >= 0), others, -1)
    first = block_ids - 1
    return jnp.concatenate([first[:, None], others], axis=1).astype(jnp.int32)


def draw_whiten(key, part):
    key = jax.random.fold_in(key, 5)
    key_diagonal, key_lower = jax.random.split(key)
    diagonal = jnp.exp(jax.random.uniform(key_diagonal, (NBLK, PTS), minval=math.log(0.5), maxval=math.log(2.0)))
    lower = jax.random.normal(key_lower, (NBLK, PTS, PTS))
    lower = lower * (0.6 / math.sqrt(PTS))
    row_index = jnp.arange(PTS)[:, None]
    col_index = jnp.arange(PTS)[None, :]
    values = jnp.where(row_index > col_index, lower, 0.0)
    values = values + jnp.where(row_index == col_index, 1.0, 0.0)[None, :, :] * diagonal[:, :, None]
    return jnp.clip(values, -1.0, 2.0).astype(jnp.bfloat16)


def strengthened(result, key, source, target, blocks, factor):
    owner, partner = [(jnp.arange(result.shape[axis_at]) // (result.shape[axis_at] // blocks)).reshape([-1 if axis == axis_at else 1 for axis in range(result.ndim)]) for axis_at in (source, target)]
    chosen = jax.random.permutation(key, blocks)[partner]
    strong = (owner == chosen) | (owner == (partner + blocks // 2) % blocks)
    return jnp.where(strong, factor * result, result)


def block_scale(key, extent, cuts, least, top_value):
    factor_of = 1.0
    for axis_at, blocks in cuts:
        steps = jax.random.uniform(jax.random.fold_in(jax.random.fold_in(key, 6), axis_at), (blocks,), jnp.float32, least / len(cuts), top_value / len(cuts))
        factor_of = factor_of * jnp.repeat(jnp.exp(steps), extent[axis_at] // blocks).reshape((-1,) + (1,) * (len(extent) - 1 - axis_at))
    return factor_of


def gaussian(key, extent, width, limit, cuts=(), kind=jnp.bfloat16):
    gain = block_scale(key, extent, cuts, -0.22, 0.18) if cuts else 1.0
    result = jax.random.normal(key, extent, jnp.float32) * width * gain
    return jnp.minimum(jnp.maximum(result, -limit), limit).astype(kind)


def heavy_noise(stream_key, shape, scale, bound, pieces, heavy, kind=jnp.bfloat16):
    array = scale * jax.random.normal(stream_key, shape, jnp.float32)
    if pieces:
        array = array * block_scale(stream_key, shape, pieces, -0.22, 0.18)
    return jnp.clip(strengthened(array, jax.random.fold_in(stream_key, 3), *heavy), -bound, bound).astype(kind)


def setup_inputs(seed: int = 0, part: int = 0) -> dict:
    splits = jax.random.split(jax.random.key(seed), 9)
    part_splits = jax.random.split(jax.random.fold_in(splits[8], part), 9)
    obs = draw_obs(jax.random.fold_in(jax.random.fold_in(splits[8], part), 71), part)
    counts = draw_counts(jax.random.fold_in(jax.random.fold_in(splits[8], part), 71), part)
    neighbours = draw_neighbours(jax.random.fold_in(jax.random.fold_in(splits[8], part), 71), part)
    krig = gaussian(part_splits[3], (NBLK, NEIGH, PTS, PTS), (NEIGH * PTS) ** -0.5, 0.1875, ((0, 16),))
    knot_load = heavy_noise(part_splits[4], (NBLK, PTS, KNOTS), KNOTS ** -0.5, 0.1875, ((0, 16),), (0, 2, 16, 2.0))
    knot_values = gaussian(part_splits[5], (KNOTS, FIELDS), 1.0, 6.0, ((0, 16),))
    whiten = draw_whiten(jax.random.fold_in(jax.random.fold_in(splits[8], part), 71), part)
    noise_var = jnp.clip(jnp.exp(jax.random.uniform(splits[7], (FIELDS,), jnp.float32, math.log(0.2), math.log(1.0))), 0.2, 1.0)
    return {"obs": obs, "counts": counts, "neighbours": neighbours, "krig": krig, "knot_load": knot_load, "knot_values": knot_values, "whiten": whiten, "noise_var": noise_var}


def reference(obs, counts, neighbours, krig, knot_load, knot_values, whiten, noise_var):
    point_count = obs.shape[1]
    field_count = obs.shape[2]
    knot_count = knot_load.shape[2]
    point_mask = (jnp.arange(point_count)[None, :] < counts[:, None]).astype(jnp.float32)
    spread_mask = point_mask[:, :, None]
    masked = (obs.astype(jnp.float32) * spread_mask).astype(jnp.bfloat16)
    usable = neighbours >= 0
    safe_ids = jnp.where(usable, neighbours, 0).astype(jnp.int32)
    predicted = jnp.zeros(obs.shape, jnp.float32)
    for column in range(NEIGH):
        near_rows = jnp.where(usable[:, column, None, None], masked[safe_ids[:, column]], jnp.zeros((), jnp.bfloat16))
        predicted = predicted + jnp.einsum("bij,bjt->bit", krig[:, column].astype(jnp.float32), near_rows.astype(jnp.float32))
    flat_load = knot_load.reshape(-1, knot_count)
    coarse = jnp.dot(flat_load, knot_values, preferred_element_type=jnp.float32).reshape(obs.shape)
    residual = (spread_mask * (masked.astype(jnp.float32) - predicted - coarse)).astype(jnp.bfloat16)
    whiten_wide = whiten.astype(jnp.float32)
    whitened = spread_mask * jnp.einsum("bij,bjt->bit", whiten_wide, residual.astype(jnp.float32))
    whitened_half = whitened.astype(jnp.bfloat16)
    adjoint = spread_mask * jnp.einsum("bji,bjt->bit", whiten_wide, whitened_half.astype(jnp.float32))
    adjoint_half = adjoint.astype(jnp.bfloat16)
    diagonal = jnp.diagonal(whiten, axis1=1, axis2=2).astype(jnp.float32)
    log_total = jnp.sum(point_mask * jnp.log(diagonal))
    squares = jnp.sum(whitened * whitened, axis=(0, 1))
    average_loglik = (log_total - 0.5 * squares) / jnp.sum(counts).astype(jnp.float32)
    knot_score = jnp.dot(flat_load.T, adjoint_half.reshape(-1, field_count), preferred_element_type=jnp.float32)
    transposed = jnp.stack([jnp.einsum("bij,bit->bjt", krig[:, column].astype(jnp.float32), adjoint_half.astype(jnp.float32)) for column in range(NEIGH)], axis=1)
    target_ids = jnp.where(usable, neighbours, NBLK).astype(jnp.int32)

    def tile_step(running, tile):
        first_block = (tile * SLOTS).astype(jnp.int32)
        tile_terms = lax.dynamic_slice_in_dim(transposed, first_block, SLOTS, 0)
        tile_targets = lax.dynamic_slice_in_dim(target_ids, first_block, SLOTS, 0)
        buffer_sums = jnp.zeros(obs.shape, jnp.float32).at[tile_targets.reshape(-1)].add(
            tile_terms.reshape(-1, point_count, field_count), mode="drop")
        returned = lax.optimization_barrier(buffer_sums.astype(jnp.bfloat16))
        return running + returned.astype(jnp.float32), None

    incoming, _ = lax.scan(tile_step, jnp.zeros(obs.shape, jnp.float32), jnp.arange(N_SPACE, dtype=jnp.int32))
    precision_resid = spread_mask * (adjoint - incoming)
    posterior = (masked.astype(jnp.float32) - noise_var[None, None, :] * precision_resid).astype(jnp.bfloat16)
    return posterior, average_loglik, knot_score
```

```python
import functools

import jax
import jax.numpy as jnp
from jax import lax
from jax.experimental import pallas as pl
from jax.experimental.pallas import tpu as pltpu
from jax.sharding import PartitionSpec as P

REACH = 9
VMEM_LIMIT = 56 * 1024 * 1024
F32 = jnp.float32
BF16 = jnp.bfloat16


def remote(src, dst, send_sem, recv_sem, target):
    return pltpu.make_async_remote_copy(
        src_ref=src,
        dst_ref=dst,
        send_sem=send_sem,
        recv_sem=recv_sem,
        device_id={"space": target},
        device_id_type=pl.DeviceIdType.MESH,
    )


def flip(i, bit):
    size = 1 << bit
    return i + size - 2 * size * ((i // size) % 2)


def greet(i, n, bits):
    barrier = pltpu.get_barrier_semaphore()
    others = [flip(i, bit) for bit in range(bits)]
    others += [lax.rem(i + by, n) for by in (1, 2, n - 1, n - 2)]
    for other in others:
        pl.semaphore_signal(
            barrier, inc=1, device_id={"space": other}, device_id_type=pl.DeviceIdType.MESH
        )
    pl.semaphore_wait(barrier, len(others))


def row_mask(points, count):
    return (lax.broadcasted_iota(jnp.int32, (points, 1), 0) < count).astype(F32)


def gather_kernel(
    n, bits, counts, obs, load, values, window, base, obs_v, load_v, knots,
    obs_sem, load_sem, near_send, near_recv, far_send, far_recv, pass_send, knot_send, knot_recv,
):
    i = lax.axis_index("space")
    slots, points, fields = obs_v.shape
    far = REACH - slots
    rows = values.shape[0]
    obs_copies = [pltpu.make_async_copy(obs.at[s], obs_v.at[s], obs_sem.at[s]) for s in range(slots)]
    load_copies = [pltpu.make_async_copy(load.at[s], load_v.at[s], load_sem.at[s]) for s in range(slots)]
    for s in reversed(range(slots)):
        obs_copies[s].start()
    for s in range(slots):
        load_copies[s].start()

    def chunk(j):
        return knots.at[pl.ds(pl.multiple_of(j * rows, rows), rows)]

    knots[pl.ds(pl.multiple_of(i * rows, rows), rows), :] = values[...]
    greet(i, n, bits)

    def gather_step(t):
        bit = bits - 1 - t
        stride = 2 << bit
        partner = flip(i, bit)
        sends, receives = [], []
        for m in range(n // stride):
            at = (1 << t) - 1 + m
            mine = chunk(lax.rem(i, stride) + m * stride)
            theirs = chunk(lax.rem(partner, stride) + m * stride)
            sends.append(remote(mine, mine, knot_send.at[at], knot_recv.at[at], partner))
            receives.append(remote(theirs, theirs, knot_send.at[at], knot_recv.at[at], partner))
        return sends, receives

    steps = [gather_step(t) for t in range(bits)]
    for copy in steps[0][0]:
        copy.start()

    def near_copy(s, to):
        return remote(window.at[REACH + s], window.at[far + s], near_send.at[s], near_recv.at[s], to)

    def far_copy(q, to):
        return remote(window.at[REACH + slots - far + q], window.at[q], far_send.at[q], far_recv.at[q], to)

    def pass_copy(q, to):
        return remote(window.at[REACH - far + q], window.at[q], pass_send.at[q], far_recv.at[q], to)

    even = lax.rem(i, 2) == 0
    has_next = i < n - 1
    sends_far = jnp.logical_and(even, i < n - 2)
    passes = jnp.logical_and(even, i > 0)
    next_one, next_two = lax.rem(i + 1, n), lax.rem(i + 2, n)

    for s in reversed(range(slots)):
        obs_copies[s].wait()
        window[REACH + s] = (obs_v[s].astype(F32) * row_mask(points, counts[s])).astype(BF16)

        @pl.when(has_next)
        def _():
            near_copy(s, next_one).start()

        if s >= slots - far:

            @pl.when(sends_far)
            def _():
                far_copy(s - (slots - far), next_two).start()

    for t in range(bits):
        for copy in steps[t][1]:
            copy.wait_recv()
        if t + 1 < bits:
            for copy in steps[t + 1][0]:
                copy.start()

    for q in reversed(range(far)):

        @pl.when(i > 0)
        def _():
            near_copy(slots - far + q, next_one).wait_recv()

        @pl.when(passes)
        def _():
            pass_copy(q, next_one).start()

    for s in range(slots):
        load_copies[s].wait()

    def coarse_step(s, carry):
        coarse = jnp.dot(load_v[s], knots[...], preferred_element_type=F32)
        base[s] = window[REACH + s].astype(F32) - coarse
        return carry

    lax.fori_loop(0, slots, coarse_step, 0)

    @pl.when(i > 0)
    def _():
        for s in range(slots - far):
            near_copy(s, next_one).wait_recv()

    @pl.when(i > 1)
    def _():
        for q in range(far):
            far_copy(q, next_two).wait_recv()

    @pl.when(has_next)
    def _():
        for s in range(slots):
            near_copy(s, next_one).wait_send()

    @pl.when(sends_far)
    def _():
        for q in range(far):
            far_copy(q, next_two).wait_send()

    @pl.when(passes)
    def _():
        for q in range(far):
            pass_copy(q, next_one).wait_send()

    for sends, _ in steps:
        for copy in sends:
            copy.wait_send()


def block_kernel(
    near, counts, window, base, krig, whiten, returned, adjoint_half, rest, stats, sums, adjoints
):
    s = pl.program_id(0)
    slots = pl.num_programs(0)
    neigh, points = krig.shape[1], krig.shape[2]
    window_length = window.shape[0]
    count = counts[s]
    mask = row_mask(points, count)

    @pl.when(s == 0)
    def _():
        sums[...] = jnp.zeros_like(sums)
        stats[...] = jnp.zeros_like(stats)

    predicted = None
    for k in range(neigh):
        at = near[s * neigh + k]
        block = jnp.where(at >= 0, krig[0, k], jnp.zeros((), BF16))
        term = jnp.dot(block, window[jnp.where(at >= 0, at, REACH)], preferred_element_type=F32)
        predicted = term if predicted is None else predicted + term
    factor = whiten[0]
    residual = (mask * (base[0] - predicted)).astype(BF16)
    whitened = mask * jnp.dot(factor, residual, preferred_element_type=F32)
    adjoint = mask * lax.dot_general(
        factor, whitened.astype(BF16), (((0,), (0,)), ((), ())), preferred_element_type=F32
    )
    half = adjoint.astype(BF16)
    adjoint_half[0] = half
    adjoints[s] = adjoint
    diagonal_at = lax.broadcasted_iota(jnp.int32, (points, points), 0) == lax.broadcasted_iota(
        jnp.int32, (points, points), 1
    )
    diagonal = jnp.sum(jnp.where(diagonal_at, factor.astype(F32), 0.0), axis=1, keepdims=True)
    stats[0:1] += jnp.sum(whitened * whitened, axis=0, keepdims=True)
    stats[1:2] += jnp.sum(mask * jnp.log(diagonal), axis=0, keepdims=True)
    stats[2:3] += jnp.full((1, stats.shape[1]), count.astype(F32))
    for k in range(neigh):
        at = near[s * neigh + k]
        to = jnp.where(at >= 0, at, window_length)
        sums[to] += lax.dot_general(
            krig[0, k], half, (((0,), (0,)), ((), ())), preferred_element_type=F32
        )

    @pl.when(s == slots - 1)
    def _():
        def emit(c, carry):
            returned[c] = sums[c].astype(BF16)
            return carry

        def keep(c, carry):
            rest[c] = adjoints[c] - sums[REACH + c].astype(BF16).astype(F32)
            return carry

        lax.fori_loop(0, REACH, emit, 0)
        lax.fori_loop(0, window_length - REACH, keep, 0)


def score_kernel(
    n, bits, counts, noise, stats, half, returned, rest, window, load,
    posterior, loglik, score,
    load_v, rest_v, masked_v, near_v, far_v, partial, landed, stat_v, stat_in,
    local_sem, near_send, near_recv, far_send, far_recv, part_send, part_recv, stat_send, stat_recv,
):
    i = lax.axis_index("space")
    slots, points, fields = rest_v.shape
    far = REACH - slots
    rows = score.shape[0]
    knot_count = partial.shape[0]
    load_copy = pltpu.make_async_copy(load, load_v, local_sem.at[0])
    rest_copy = pltpu.make_async_copy(rest, rest_v, local_sem.at[1])
    masked_copy = pltpu.make_async_copy(window.at[pl.ds(REACH, slots)], masked_v, local_sem.at[2])
    load_copy.start()
    stat_v[0] = stats[...]
    greet(i, n, bits)

    def near_copy(s):
        return remote(
            returned.at[far + s], near_v.at[s], near_send.at[s], near_recv.at[s], lax.rem(i + n - 1, n)
        )

    def far_copy(q):
        return remote(returned.at[q], far_v.at[q], far_send.at[q], far_recv.at[q], lax.rem(i + n - 2, n))

    @pl.when(i > 0)
    def _():
        for s in range(slots):
            near_copy(s).start()

    @pl.when(i > 1)
    def _():
        for q in range(far):
            far_copy(q).start()

    def stat_copy(t):
        return remote(stat_v.at[t], stat_in.at[t], stat_send.at[t], stat_recv.at[t], flip(i, t))

    def piece(j):
        return pl.ds(pl.multiple_of(j * rows, rows), rows)

    def start_of(t):
        return n - (n >> t)

    def part_copy(t, j, m):
        at = start_of(t) + m
        return remote(
            partial.at[piece(j)], landed.at[at], part_send.at[at], part_recv.at[at], flip(i, t)
        )

    stat_copy(0).start()
    load_copy.wait()
    rest_copy.start()
    masked_copy.start()

    tile = min(256, knot_count)
    pairs = tile // rows // 2
    other = 1 - lax.rem(i, 2)

    def tile_step(u, carry):
        at = pl.multiple_of(u * tile, tile)
        partial[pl.ds(at, tile), :] = lax.dot_general(
            load_v[:, pl.ds(at, tile)], half[...], (((0,), (0,)), ((), ())), preferred_element_type=F32
        )
        for q in range(pairs):
            m = u * pairs + q
            part_copy(0, 2 * m + other, m).start()
        return carry

    lax.fori_loop(0, knot_count // tile, tile_step, 0)

    def settle(j, steps):
        for t in range(steps):
            m = j // (2 << t)
            at = start_of(t) + m
            part_copy(t, j, m).wait_recv()
            partial[piece(j), :] += landed[at]

    for t in range(1, bits + 1):
        stat_copy(t - 1).wait_recv()
        stat_v[t] = stat_v[t - 1] + stat_in[t - 1]
        if t < bits:
            stat_copy(t).start()
            low = lax.rem(flip(i, t), 2 << t)
            for m in range(n >> (t + 1)):
                j = low + m * (2 << t)
                settle(j, t)
                part_copy(t, j, m).start()
    settle(i, bits)
    score[...] = partial[piece(i), :]
    totals = stat_v[bits]
    loglik[...] = (totals[1:2] - 0.5 * totals[0:1]) / totals[2:3]

    rest_copy.wait()
    masked_copy.wait()
    for s in reversed(range(slots)):

        @pl.when(i < n - 1)
        def _():
            near_copy(s).wait_recv()
            rest_v[s] = rest_v[s] - near_v[s].astype(F32)

        if s >= slots - far:

            @pl.when(i < n - 2)
            def _():
                far_copy(s - (slots - far)).wait_recv()
                rest_v[s] = rest_v[s] - far_v[s - (slots - far)].astype(F32)

        precision = row_mask(points, counts[s]) * rest_v[s]
        posterior[s] = (masked_v[s].astype(F32) - noise[...] * precision).astype(BF16)

    @pl.when(i > 0)
    def _():
        for s in range(slots):
            near_copy(s).wait_send()

    @pl.when(i > 1)
    def _():
        for q in range(far):
            far_copy(q).wait_send()

    for t in range(bits):
        stat_copy(t).wait_send()
        low = lax.rem(flip(i, t), 2 << t)
        for m in range(n >> (t + 1)):
            part_copy(t, low + m * (2 << t), m).wait_send()


def vmem():
    return pl.BlockSpec(memory_space=pltpu.VMEM)


def smem():
    return pl.BlockSpec(memory_space=pltpu.SMEM)


def anywhere():
    return pl.BlockSpec(memory_space=pl.ANY)


def local(n, obs, counts, neighbours, krig, knot_load, knot_values, whiten, noise_var):
    bits = n.bit_length() - 1
    slots, points, fields = obs.shape
    knot_count = knot_load.shape[2]
    neigh = neighbours.shape[1]
    far = REACH - slots
    window_length = REACH + slots
    rows = knot_values.shape[0]
    dma = pltpu.SemaphoreType.DMA

    window, base = pl.pallas_call(
        functools.partial(gather_kernel, n, bits),
        out_shape=(
            jax.ShapeDtypeStruct((window_length, points, fields), BF16),
            jax.ShapeDtypeStruct((slots, points, fields), F32),
        ),
        in_specs=[smem(), anywhere(), anywhere(), vmem()],
        out_specs=(vmem(), vmem()),
        scratch_shapes=[
            pltpu.VMEM((slots, points, fields), BF16),
            pltpu.VMEM((slots, points, knot_count), BF16),
            pltpu.VMEM((knot_count, fields), BF16),
            dma((slots,)), dma((slots,)), dma((slots,)), dma((slots,)),
            dma((far,)), dma((far,)), dma((far,)), dma((n - 1,)), dma((n - 1,)),
        ],
        compiler_params=pltpu.CompilerParams(
            collective_id=0, has_side_effects=True, vmem_limit_bytes=VMEM_LIMIT
        ),
    )(counts, obs, knot_load, knot_values)

    anchor = lax.axis_index("space") * slots - REACH
    near = jnp.where(neighbours >= 0, neighbours - anchor, -1).reshape(-1)

    def whole(*shape):
        return pl.BlockSpec(shape, lambda s, *_: (0,) * len(shape))

    def slot(*shape):
        return pl.BlockSpec((1,) + shape, lambda s, *_: (s,) + (0,) * len(shape))

    returned, adjoint_half, rest, stats = pl.pallas_call(
        block_kernel,
        out_shape=(
            jax.ShapeDtypeStruct((REACH, points, fields), BF16),
            jax.ShapeDtypeStruct((slots, points, fields), BF16),
            jax.ShapeDtypeStruct((slots, points, fields), F32),
            jax.ShapeDtypeStruct((8, fields), F32),
        ),
        grid_spec=pltpu.PrefetchScalarGridSpec(
            num_scalar_prefetch=2,
            grid=(slots,),
            in_specs=[
                whole(window_length, points, fields),
                slot(points, fields),
                slot(neigh, points, points),
                slot(points, points),
            ],
            out_specs=(
                whole(REACH, points, fields),
                slot(points, fields),
                whole(slots, points, fields),
                whole(8, fields),
            ),
            scratch_shapes=[
                pltpu.VMEM((window_length + 1, points, fields), F32),
                pltpu.VMEM((slots, points, fields), F32),
            ],
        ),
        compiler_params=pltpu.CompilerParams(
            dimension_semantics=("arbitrary",), vmem_limit_bytes=VMEM_LIMIT
        ),
    )(near, counts, window, base, krig, whiten)

    posterior, loglik, score = pl.pallas_call(
        functools.partial(score_kernel, n, bits),
        out_shape=(
            jax.ShapeDtypeStruct((slots, points, fields), BF16),
            jax.ShapeDtypeStruct((1, fields), F32),
            jax.ShapeDtypeStruct((rows, fields), F32),
        ),
        in_specs=[smem(), vmem(), vmem(), vmem(), anywhere(), anywhere(), anywhere(), anywhere()],
        out_specs=(vmem(), vmem(), vmem()),
        scratch_shapes=[
            pltpu.VMEM((slots * points, knot_count), BF16),
            pltpu.VMEM((slots, points, fields), F32),
            pltpu.VMEM((slots, points, fields), BF16),
            pltpu.VMEM((slots, points, fields), BF16),
            pltpu.VMEM((far, points, fields), BF16),
            pltpu.VMEM((knot_count, fields), F32),
            pltpu.VMEM((n - 1, rows, fields), F32),
            pltpu.VMEM((bits + 1, 8, fields), F32),
            pltpu.VMEM((bits, 8, fields), F32),
            dma((3,)), dma((slots,)), dma((slots,)), dma((far,)), dma((far,)),
            dma((n - 1,)), dma((n - 1,)), dma((bits,)), dma((bits,)),
        ],
        compiler_params=pltpu.CompilerParams(
            collective_id=1, has_side_effects=True, vmem_limit_bytes=VMEM_LIMIT
        ),
    )(
        counts,
        noise_var[None, :],
        stats,
        adjoint_half.reshape(slots * points, fields),
        returned,
        rest,
        window,
        knot_load.reshape(slots * points, knot_count),
    )
    return posterior, loglik.reshape(fields), score


def solution(mesh):
    in_specs = (
        P(("parts", "space"), None, None),
        P(("parts", "space")),
        P(("parts", "space"), None),
        P(("parts", "space"), None, None, None),
        P(("parts", "space"), None, None),
        P(("parts", "space"), None),
        P(("parts", "space"), None, None),
        P(),
    )
    out_specs = (P(("parts", "space"), None, None), P("parts"), P(("parts", "space"), None))
    return jax.shard_map(
        functools.partial(local, mesh.shape["space"]),
        mesh=mesh,
        in_specs=in_specs,
        out_specs=out_specs,
        check_vma=False,
    )
```

```python
import functools

import jax
import jax.numpy as jnp
from jax import lax
from jax.experimental import pallas as pl
from jax.experimental.pallas import tpu as pltpu
from jax.sharding import PartitionSpec as P

REACH = 9
VMEM_LIMIT = 56 * 1024 * 1024
F32 = jnp.float32
BF16 = jnp.bfloat16


def remote(src, dst, send_sem, recv_sem, target):
    return pltpu.make_async_remote_copy(
        src_ref=src,
        dst_ref=dst,
        send_sem=send_sem,
        recv_sem=recv_sem,
        device_id={"space": target},
        device_id_type=pl.DeviceIdType.MESH,
    )


def flip(i, bit):
    size = 1 << bit
    return i + size - 2 * size * ((i // size) % 2)


def greet(i, n, bits):
    barrier = pltpu.get_barrier_semaphore()
    others = [flip(i, bit) for bit in range(bits)]
    others += [lax.rem(i + by, n) for by in (1, 2, n - 1, n - 2)]
    for other in others:
        pl.semaphore_signal(
            barrier, inc=1, device_id={"space": other}, device_id_type=pl.DeviceIdType.MESH
        )
    pl.semaphore_wait(barrier, len(others))


def row_mask(points, count):
    return (lax.broadcasted_iota(jnp.int32, (points, 1), 0) < count).astype(F32)


def gather_kernel(
    n, bits, counts, obs, load, values, window, base, obs_v, load_v, knots,
    obs_sem, load_sem, near_send, near_recv, far_send, far_recv, pass_send, knot_send, knot_recv,
):
    i = lax.axis_index("space")
    slots, points, fields = obs_v.shape
    far = REACH - slots
    rows = values.shape[0]
    obs_copies = [pltpu.make_async_copy(obs.at[s], obs_v.at[s], obs_sem.at[s]) for s in range(slots)]
    load_copies = [pltpu.make_async_copy(load.at[s], load_v.at[s], load_sem.at[s]) for s in range(slots)]
    for s in reversed(range(slots)):
        obs_copies[s].start()
    for s in range(slots):
        load_copies[s].start()

    def chunk(j):
        return knots.at[pl.ds(pl.multiple_of(j * rows, rows), rows)]

    knots[pl.ds(pl.multiple_of(i * rows, rows), rows), :] = values[...]
    greet(i, n, bits)

    def gather_step(t):
        bit = bits - 1 - t
        stride = 2 << bit
        partner = flip(i, bit)
        sends, receives = [], []
        for m in range(n // stride):
            at = (1 << t) - 1 + m
            mine = chunk(lax.rem(i, stride) + m * stride)
            theirs = chunk(lax.rem(partner, stride) + m * stride)
            sends.append(remote(mine, mine, knot_send.at[at], knot_recv.at[at], partner))
            receives.append(remote(theirs, theirs, knot_send.at[at], knot_recv.at[at], partner))
        return sends, receives

    steps = [gather_step(t) for t in range(bits)]
    for copy in steps[0][0]:
        copy.start()

    def near_copy(s, to):
        return remote(window.at[REACH + s], window.at[far + s], near_send.at[s], near_recv.at[s], to)

    def far_copy(q, to):
        return remote(window.at[REACH + slots - far + q], window.at[q], far_send.at[q], far_recv.at[q], to)

    def pass_copy(q, to):
        return remote(window.at[REACH - far + q], window.at[q], pass_send.at[q], far_recv.at[q], to)

    even = lax.rem(i, 2) == 0
    has_next = i < n - 1
    sends_far = jnp.logical_and(even, i < n - 2)
    passes = jnp.logical_and(even, i > 0)
    next_one, next_two = lax.rem(i + 1, n), lax.rem(i + 2, n)

    for s in reversed(range(slots)):
        obs_copies[s].wait()
        window[REACH + s] = (obs_v[s].astype(F32) * row_mask(points, counts[s])).astype(BF16)

        if s >= slots - far:

            @pl.when(has_next)
            def _():
                near_copy(s, next_one).start()

    for t in range(bits):
        for copy in steps[t][1]:
            copy.wait_recv()
        if t + 1 < bits:
            for copy in steps[t + 1][0]:
                copy.start()
        if t == bits - 2:

            @pl.when(sends_far)
            def _():
                for q in reversed(range(far)):
                    far_copy(q, next_two).start()

            @pl.when(has_next)
            def _():
                for s in reversed(range(slots - far)):
                    near_copy(s, next_one).start()

    for q in reversed(range(far)):

        @pl.when(i > 0)
        def _():
            near_copy(slots - far + q, next_one).wait_recv()

        @pl.when(passes)
        def _():
            pass_copy(q, next_one).start()

    for s in range(slots):
        load_copies[s].wait()

    def coarse_step(s, carry):
        coarse = jnp.dot(load_v[s], knots[...], preferred_element_type=F32)
        base[s] = window[REACH + s].astype(F32) - coarse
        return carry

    lax.fori_loop(0, slots, coarse_step, 0)

    @pl.when(i > 0)
    def _():
        for s in range(slots - far):
            near_copy(s, next_one).wait_recv()

    @pl.when(i > 1)
    def _():
        for q in range(far):
            far_copy(q, next_two).wait_recv()

    @pl.when(has_next)
    def _():
        for s in range(slots):
            near_copy(s, next_one).wait_send()

    @pl.when(sends_far)
    def _():
        for q in range(far):
            far_copy(q, next_two).wait_send()

    @pl.when(passes)
    def _():
        for q in range(far):
            pass_copy(q, next_one).wait_send()

    for sends, _ in steps:
        for copy in sends:
            copy.wait_send()


def block_kernel(
    near, counts, window, base, krig, whiten, returned, adjoint_half, rest, stats, sums, adjoints
):
    step = pl.program_id(0)
    group, neigh, points = krig.shape[0], krig.shape[1], krig.shape[2]
    window_length = window.shape[0]
    slots = window_length - REACH
    anchor = lax.axis_index("space") * slots - REACH
    members = range(group)
    ids = [step * group + g for g in members]
    masks = [row_mask(points, counts[s]) for s in ids]

    @pl.when(step == 0)
    def _():
        sums[...] = jnp.zeros_like(sums)
        stats[...] = jnp.zeros_like(stats)

    places = [[near[s, k] - anchor for k in range(neigh)] for s in ids]
    valid = [[near[s, k] >= 0 for k in range(neigh)] for s in ids]
    predicted = []
    for g in members:
        total = None
        for k in range(neigh):
            block = jnp.where(valid[g][k], krig[g, k], jnp.zeros((), BF16))
            rows = window[jnp.where(valid[g][k], places[g][k], REACH)]
            term = jnp.dot(block, rows, preferred_element_type=F32)
            total = term if total is None else total + term
        predicted.append(total)
    residual = [(masks[g] * (base[g] - predicted[g])).astype(BF16) for g in members]
    whitened = [
        masks[g] * jnp.dot(whiten[g], residual[g], preferred_element_type=F32) for g in members
    ]
    whitened_half = [w.astype(BF16) for w in whitened]
    adjoint = [
        masks[g]
        * lax.dot_general(
            whiten[g], whitened_half[g], (((0,), (0,)), ((), ())), preferred_element_type=F32
        )
        for g in members
    ]
    half = [a.astype(BF16) for a in adjoint]
    for g in members:
        adjoint_half[g] = half[g]
        adjoints[ids[g]] = adjoint[g]
    for g in members:
        for k in range(neigh):
            to = jnp.where(valid[g][k], places[g][k], window_length)
            sums[to] += lax.dot_general(
                krig[g, k], half[g], (((0,), (0,)), ((), ())), preferred_element_type=F32
            )
    diagonal_at = lax.broadcasted_iota(jnp.int32, (points, points), 0) == lax.broadcasted_iota(
        jnp.int32, (points, points), 1
    )
    for g in members:
        diagonal = jnp.sum(
            jnp.where(diagonal_at, whiten[g].astype(F32), 0.0), axis=1, keepdims=True
        )
        stats[0:1] += jnp.sum(whitened[g] * whitened[g], axis=0, keepdims=True)
        stats[1:2] += jnp.sum(masks[g] * jnp.log(diagonal), axis=0, keepdims=True)
        stats[2:3] += jnp.full((1, stats.shape[1]), counts[ids[g]].astype(F32))

    @pl.when(step == pl.num_programs(0) - 1)
    def _():
        def emit(c, carry):
            returned[c] = sums[c].astype(BF16)
            return carry

        def keep(c, carry):
            rest[c] = adjoints[c] - sums[REACH + c].astype(BF16).astype(F32)
            return carry

        lax.fori_loop(0, REACH, emit, 0)
        lax.fori_loop(0, slots, keep, 0)


def score_kernel(
    n, bits, counts, noise, stats, half, returned, rest, window, load,
    posterior, loglik, score,
    load_v, rest_v, masked_v, near_v, far_v, partial, landed, stat_v, stat_in,
    local_sem, near_send, near_recv, far_send, far_recv, part_send, part_recv, stat_send, stat_recv,
):
    i = lax.axis_index("space")
    slots, points, fields = rest_v.shape
    far = REACH - slots
    rows = score.shape[0]
    knot_count = partial.shape[0]
    load_copy = pltpu.make_async_copy(load, load_v, local_sem.at[0])
    rest_copy = pltpu.make_async_copy(rest, rest_v, local_sem.at[1])
    masked_copy = pltpu.make_async_copy(window.at[pl.ds(REACH, slots)], masked_v, local_sem.at[2])
    load_copy.start()
    stat_v[0] = stats[...]
    greet(i, n, bits)

    def near_copy(s):
        return remote(
            returned.at[far + s], near_v.at[s], near_send.at[s], near_recv.at[s], lax.rem(i + n - 1, n)
        )

    def far_copy(q):
        return remote(returned.at[q], far_v.at[q], far_send.at[q], far_recv.at[q], lax.rem(i + n - 2, n))

    @pl.when(i > 1)
    def _():
        for q in range(far):
            far_copy(q).start()

    def stat_copy(t):
        return remote(stat_v.at[t], stat_in.at[t], stat_send.at[t], stat_recv.at[t], flip(i, t))

    def piece(j):
        return pl.ds(pl.multiple_of(j * rows, rows), rows)

    def start_of(t):
        return n - (n >> t)

    def part_copy(t, j, m):
        at = start_of(t) + m
        return remote(
            partial.at[piece(j)], landed.at[at], part_send.at[at], part_recv.at[at], flip(i, t)
        )

    stat_copy(0).start()
    load_copy.wait()
    rest_copy.start()
    masked_copy.start()

    tile = min(256, knot_count)
    pairs = tile // rows // 2
    other = 1 - lax.rem(i, 2)

    def tile_step(u, carry):
        at = pl.multiple_of(u * tile, tile)
        partial[pl.ds(at, tile), :] = lax.dot_general(
            load_v[:, pl.ds(at, tile)], half[...], (((0,), (0,)), ((), ())), preferred_element_type=F32
        )
        for q in range(pairs):
            m = u * pairs + q
            part_copy(0, 2 * m + other, m).start()
        return carry

    lax.fori_loop(0, knot_count // tile, tile_step, 0)

    def settle(j, steps):
        for t in range(steps):
            m = j // (2 << t)
            at = start_of(t) + m
            part_copy(t, j, m).wait_recv()
            partial[piece(j), :] += landed[at]

    for t in range(1, bits + 1):
        stat_copy(t - 1).wait_recv()
        stat_v[t] = stat_v[t - 1] + stat_in[t - 1]
        if t < bits:
            stat_copy(t).start()
            low = lax.rem(flip(i, t), 2 << t)
            for m in range(n >> (t + 1)):
                j = low + m * (2 << t)
                settle(j, t)
                part_copy(t, j, m).start()
        if t == 2:

            @pl.when(i > 0)
            def _():
                for s in reversed(range(slots)):
                    near_copy(s).start()

    settle(i, bits)
    score[...] = partial[piece(i), :]
    totals = stat_v[bits]
    loglik[...] = (totals[1:2] - 0.5 * totals[0:1]) / totals[2:3]

    rest_copy.wait()
    masked_copy.wait()
    for s in reversed(range(slots)):

        @pl.when(i < n - 1)
        def _():
            near_copy(s).wait_recv()
            rest_v[s] = rest_v[s] - near_v[s].astype(F32)

        if s >= slots - far:

            @pl.when(i < n - 2)
            def _():
                far_copy(s - (slots - far)).wait_recv()
                rest_v[s] = rest_v[s] - far_v[s - (slots - far)].astype(F32)

        precision = row_mask(points, counts[s]) * rest_v[s]
        posterior[s] = (masked_v[s].astype(F32) - noise[...] * precision).astype(BF16)

    @pl.when(i > 0)
    def _():
        for s in range(slots):
            near_copy(s).wait_send()

    @pl.when(i > 1)
    def _():
        for q in range(far):
            far_copy(q).wait_send()

    for t in range(bits):
        stat_copy(t).wait_send()
        low = lax.rem(flip(i, t), 2 << t)
        for m in range(n >> (t + 1)):
            part_copy(t, low + m * (2 << t), m).wait_send()


def vmem():
    return pl.BlockSpec(memory_space=pltpu.VMEM)


def smem():
    return pl.BlockSpec(memory_space=pltpu.SMEM)


def anywhere():
    return pl.BlockSpec(memory_space=pl.ANY)


def local(n, obs, counts, neighbours, krig, knot_load, knot_values, whiten, noise_var):
    bits = n.bit_length() - 1
    slots, points, fields = obs.shape
    knot_count = knot_load.shape[2]
    neigh = neighbours.shape[1]
    far = REACH - slots
    window_length = REACH + slots
    rows = knot_values.shape[0]
    dma = pltpu.SemaphoreType.DMA

    window, base = pl.pallas_call(
        functools.partial(gather_kernel, n, bits),
        out_shape=(
            jax.ShapeDtypeStruct((window_length, points, fields), BF16),
            jax.ShapeDtypeStruct((slots, points, fields), F32),
        ),
        in_specs=[smem(), anywhere(), anywhere(), vmem()],
        out_specs=(vmem(), vmem()),
        scratch_shapes=[
            pltpu.VMEM((slots, points, fields), BF16),
            pltpu.VMEM((slots, points, knot_count), BF16),
            pltpu.VMEM((knot_count, fields), BF16),
            dma((slots,)), dma((slots,)), dma((slots,)), dma((slots,)),
            dma((far,)), dma((far,)), dma((far,)), dma((n - 1,)), dma((n - 1,)),
        ],
        compiler_params=pltpu.CompilerParams(
            collective_id=0, has_side_effects=True, vmem_limit_bytes=VMEM_LIMIT
        ),
    )(counts, obs, knot_load, knot_values)

    group = 2 - slots % 2

    def whole(*shape):
        return pl.BlockSpec(shape, lambda s, *_: (0,) * len(shape))

    def slot(*shape):
        return pl.BlockSpec((group,) + shape, lambda s, *_: (s,) + (0,) * len(shape))

    returned, adjoint_half, rest, stats = pl.pallas_call(
        block_kernel,
        out_shape=(
            jax.ShapeDtypeStruct((REACH, points, fields), BF16),
            jax.ShapeDtypeStruct((slots, points, fields), BF16),
            jax.ShapeDtypeStruct((slots, points, fields), F32),
            jax.ShapeDtypeStruct((8, fields), F32),
        ),
        grid_spec=pltpu.PrefetchScalarGridSpec(
            num_scalar_prefetch=2,
            grid=(slots // group,),
            in_specs=[
                whole(window_length, points, fields),
                slot(points, fields),
                slot(neigh, points, points),
                slot(points, points),
            ],
            out_specs=(
                whole(REACH, points, fields),
                slot(points, fields),
                whole(slots, points, fields),
                whole(8, fields),
            ),
            scratch_shapes=[
                pltpu.VMEM((window_length + 1, points, fields), F32),
                pltpu.VMEM((slots, points, fields), F32),
            ],
        ),
        compiler_params=pltpu.CompilerParams(
            dimension_semantics=("arbitrary",), vmem_limit_bytes=VMEM_LIMIT
        ),
    )(neighbours, counts, window, base, krig, whiten)

    posterior, loglik, score = pl.pallas_call(
        functools.partial(score_kernel, n, bits),
        out_shape=(
            jax.ShapeDtypeStruct((slots, points, fields), BF16),
            jax.ShapeDtypeStruct((1, fields), F32),
            jax.ShapeDtypeStruct((rows, fields), F32),
        ),
        in_specs=[smem(), vmem(), vmem(), vmem(), anywhere(), anywhere(), anywhere(), anywhere()],
        out_specs=(vmem(), vmem(), vmem()),
        scratch_shapes=[
            pltpu.VMEM((slots * points, knot_count), BF16),
            pltpu.VMEM((slots, points, fields), F32),
            pltpu.VMEM((slots, points, fields), BF16),
            pltpu.VMEM((slots, points, fields), BF16),
            pltpu.VMEM((far, points, fields), BF16),
            pltpu.VMEM((knot_count, fields), F32),
            pltpu.VMEM((n - 1, rows, fields), F32),
            pltpu.VMEM((bits + 1, 8, fields), F32),
            pltpu.VMEM((bits, 8, fields), F32),
            dma((3,)), dma((slots,)), dma((slots,)), dma((far,)), dma((far,)),
            dma((n - 1,)), dma((n - 1,)), dma((bits,)), dma((bits,)),
        ],
        compiler_params=pltpu.CompilerParams(
            collective_id=1, has_side_effects=True, vmem_limit_bytes=VMEM_LIMIT
        ),
    )(
        counts,
        noise_var[None, :],
        stats,
        adjoint_half.reshape(slots * points, fields),
        returned,
        rest,
        window,
        knot_load.reshape(slots * points, knot_count),
    )
    return posterior, loglik.reshape(fields), score


def solution(mesh):
    in_specs = (
        P(("parts", "space"), None, None),
        P(("parts", "space")),
        P(("parts", "space"), None),
        P(("parts", "space"), None, None, None),
        P(("parts", "space"), None, None),
        P(("parts", "space"), None),
        P(("parts", "space"), None, None),
        P(),
    )
    out_specs = (P(("parts", "space"), None, None), P("parts"), P(("parts", "space"), None))
    return jax.shard_map(
        functools.partial(local, mesh.shape["space"]),
        mesh=mesh,
        in_specs=in_specs,
        out_specs=out_specs,
        check_vma=False,
    )
```

```python
import functools

import jax
import jax.numpy as jnp
from jax import lax
from jax.experimental import pallas as pl
from jax.experimental.pallas import tpu as pltpu
from jax.sharding import PartitionSpec as P

REACH = 9
VMEM_LIMIT = 56 * 1024 * 1024
F32 = jnp.float32
BF16 = jnp.bfloat16


def remote(src, dst, send_sem, recv_sem, target):
    return pltpu.make_async_remote_copy(
        src_ref=src,
        dst_ref=dst,
        send_sem=send_sem,
        recv_sem=recv_sem,
        device_id={"space": target},
        device_id_type=pl.DeviceIdType.MESH,
    )


def flip(i, bit):
    size = 1 << bit
    return i + size - 2 * size * ((i // size) % 2)


def greet(i, n, bits):
    barrier = pltpu.get_barrier_semaphore()
    others = [flip(i, bit) for bit in range(bits)]
    others += [lax.rem(i + by, n) for by in (1, 2, n - 1, n - 2)]
    for other in others:
        pl.semaphore_signal(
            barrier, inc=1, device_id={"space": other}, device_id_type=pl.DeviceIdType.MESH
        )
    pl.semaphore_wait(barrier, len(others))


def row_mask(points, count):
    return (lax.broadcasted_iota(jnp.int32, (points, 1), 0) < count).astype(F32)


def gather_kernel(
    n, bits, counts, obs, load, values, window, base, obs_v, load_v, knots,
    obs_sem, load_sem, near_send, near_recv, far_send, far_recv, pass_send, knot_send, knot_recv,
):
    i = lax.axis_index("space")
    slots, points, fields = obs_v.shape
    far = REACH - slots
    rows = values.shape[0]
    obs_copies = [pltpu.make_async_copy(obs.at[s], obs_v.at[s], obs_sem.at[s]) for s in range(slots)]
    load_copies = [pltpu.make_async_copy(load.at[s], load_v.at[s], load_sem.at[s]) for s in range(slots)]
    for s in reversed(range(slots)):
        obs_copies[s].start()
    for s in range(slots):
        load_copies[s].start()

    def chunk(j):
        return knots.at[pl.ds(pl.multiple_of(j * rows, rows), rows)]

    knots[pl.ds(pl.multiple_of(i * rows, rows), rows), :] = values[...]
    greet(i, n, bits)

    def exchange(first, count, stride, mine, partner, theirs):
        sends, receives = [], []
        for m in range(count):
            at = first + m
            out, back = chunk(mine + m * stride), chunk(theirs + m * stride)
            sends.append(remote(out, out, knot_send.at[at], knot_recv.at[at], partner))
            receives.append(remote(back, back, knot_send.at[at], knot_recv.at[at], partner))
        return sends, receives

    def line_step(t):
        bit = bits - 1 - t
        stride = 2 << bit
        partner = flip(i, bit)
        return exchange(
            (1 << t) - 1, n // stride, stride, lax.rem(i, stride), partner, lax.rem(partner, stride)
        )

    def start(copies):
        for copy in copies:
            copy.start()

    lines = bits - 2
    held = n // 4
    steps = [line_step(t) for t in range(lines)]
    pair, side = flip(i, 0), flip(i, 1)
    mine, pair_low, side_low = lax.rem(i, 4), lax.rem(pair, 4), lax.rem(side, 4)
    over_pair = exchange(held - 1, held, 4, mine, pair, pair_low)
    over_side = exchange(2 * held - 1, held, 4, mine, side, side_low)
    relay = exchange(3 * held - 1, held, 4, side_low, pair, flip(side_low, 0))
    start(steps[0][0])

    def near_copy(s, to):
        return remote(window.at[REACH + s], window.at[far + s], near_send.at[s], near_recv.at[s], to)

    def far_copy(q, to):
        return remote(window.at[REACH + slots - far + q], window.at[q], far_send.at[q], far_recv.at[q], to)

    def pass_copy(q, to):
        return remote(window.at[REACH - far + q], window.at[q], pass_send.at[q], far_recv.at[q], to)

    even = lax.rem(i, 2) == 0
    has_next = i < n - 1
    sends_far = jnp.logical_and(even, i < n - 2)
    passes = jnp.logical_and(even, i > 0)
    next_one, next_two = lax.rem(i + 1, n), lax.rem(i + 2, n)

    for s in reversed(range(slots)):
        obs_copies[s].wait()
        window[REACH + s] = (obs_v[s].astype(F32) * row_mask(points, counts[s])).astype(BF16)

        @pl.when(has_next)
        def _():
            near_copy(s, next_one).start()

        if s >= slots - far:

            @pl.when(sends_far)
            def _():
                far_copy(s - (slots - far), next_two).start()

    for t in range(lines):
        for copy in steps[t][1]:
            copy.wait_recv()
        start(steps[t + 1][0] if t + 1 < lines else over_side[0] + over_pair[0])

    width = 2 * rows
    staged = width % 128 == 0

    def coarse_part(s, low):
        total = None
        for m in range(held):
            at = pl.ds(pl.multiple_of((low + 4 * m) * rows, width), width)
            term = jnp.dot(load_v[s, :, at], knots[at, :], preferred_element_type=F32)
            total = term if total is None else total + term
        return total

    for s in range(slots):
        load_copies[s].wait()
    for copy in over_pair[1]:
        copy.wait_recv()
    if staged:

        def first_step(s, carry):
            base[s] = window[REACH + s].astype(F32) - coarse_part(s, mine - lax.rem(mine, 2))
            return carry

        lax.fori_loop(0, slots, first_step, 0)

    for arrive, onward in zip(over_side[1], relay[0]):
        arrive.wait_recv()
        onward.start()

    for q in reversed(range(far)):

        @pl.when(i > 0)
        def _():
            near_copy(slots - far + q, next_one).wait_recv()

        @pl.when(passes)
        def _():
            pass_copy(q, next_one).start()

    for copy in relay[1]:
        copy.wait_recv()

    def last_step(s, carry):
        if staged:
            base[s] -= coarse_part(s, side_low - lax.rem(side_low, 2))
        else:
            coarse = jnp.dot(load_v[s], knots[...], preferred_element_type=F32)
            base[s] = window[REACH + s].astype(F32) - coarse
        return carry

    lax.fori_loop(0, slots, last_step, 0)

    @pl.when(i > 0)
    def _():
        for s in range(slots - far):
            near_copy(s, next_one).wait_recv()

    @pl.when(i > 1)
    def _():
        for q in range(far):
            far_copy(q, next_two).wait_recv()

    @pl.when(has_next)
    def _():
        for s in range(slots):
            near_copy(s, next_one).wait_send()

    @pl.when(sends_far)
    def _():
        for q in range(far):
            far_copy(q, next_two).wait_send()

    @pl.when(passes)
    def _():
        for q in range(far):
            pass_copy(q, next_one).wait_send()

    for sends, _ in steps + [over_pair, over_side, relay]:
        for copy in sends:
            copy.wait_send()


def block_kernel(
    near, counts, window, base, krig, whiten, returned, adjoint_half, rest, stats, sums, adjoints
):
    step = pl.program_id(0)
    group, neigh, points = krig.shape[0], krig.shape[1], krig.shape[2]
    window_length = window.shape[0]
    slots = window_length - REACH
    anchor = lax.axis_index("space") * slots - REACH
    members = range(group)
    ids = [step * group + g for g in members]
    masks = [row_mask(points, counts[s]) for s in ids]

    @pl.when(step == 0)
    def _():
        sums[...] = jnp.zeros_like(sums)
        stats[...] = jnp.zeros_like(stats)

    places = [[near[s, k] - anchor for k in range(neigh)] for s in ids]
    valid = [[near[s, k] >= 0 for k in range(neigh)] for s in ids]
    predicted = []
    for g in members:
        total = None
        for k in range(neigh):
            block = jnp.where(valid[g][k], krig[g, k], jnp.zeros((), BF16))
            rows = window[jnp.where(valid[g][k], places[g][k], REACH)]
            term = jnp.dot(block, rows, preferred_element_type=F32)
            total = term if total is None else total + term
        predicted.append(total)
    residual = [(masks[g] * (base[g] - predicted[g])).astype(BF16) for g in members]
    whitened = [
        masks[g] * jnp.dot(whiten[g], residual[g], preferred_element_type=F32) for g in members
    ]
    whitened_half = [w.astype(BF16) for w in whitened]
    adjoint = [
        masks[g]
        * lax.dot_general(
            whiten[g], whitened_half[g], (((0,), (0,)), ((), ())), preferred_element_type=F32
        )
        for g in members
    ]
    half = [a.astype(BF16) for a in adjoint]
    for g in members:
        adjoint_half[g] = half[g]
        adjoints[ids[g]] = adjoint[g]
    for g in members:
        for k in range(neigh):
            to = jnp.where(valid[g][k], places[g][k], window_length)
            sums[to] += lax.dot_general(
                krig[g, k], half[g], (((0,), (0,)), ((), ())), preferred_element_type=F32
            )
    diagonal_at = lax.broadcasted_iota(jnp.int32, (points, points), 0) == lax.broadcasted_iota(
        jnp.int32, (points, points), 1
    )
    for g in members:
        diagonal = jnp.sum(
            jnp.where(diagonal_at, whiten[g].astype(F32), 0.0), axis=1, keepdims=True
        )
        stats[0:1] += jnp.sum(whitened[g] * whitened[g], axis=0, keepdims=True)
        stats[1:2] += jnp.sum(masks[g] * jnp.log(diagonal), axis=0, keepdims=True)
        stats[2:3] += jnp.full((1, stats.shape[1]), counts[ids[g]].astype(F32))

    @pl.when(step == pl.num_programs(0) - 1)
    def _():
        def emit(c, carry):
            returned[c] = sums[c].astype(BF16)
            return carry

        def keep(c, carry):
            rest[c] = adjoints[c] - sums[REACH + c].astype(BF16).astype(F32)
            return carry

        lax.fori_loop(0, REACH, emit, 0)
        lax.fori_loop(0, slots, keep, 0)


def score_kernel(
    n, bits, stats, half, returned, rest, load,
    rest_v, totals, score,
    load_v, near_v, far_v, partial, landed, stat_v, stat_in,
    local_sem, near_send, near_recv, far_send, far_recv, part_send, part_recv, stat_send, stat_recv,
):
    i = lax.axis_index("space")
    slots, points, fields = rest_v.shape
    far = REACH - slots
    rows = score.shape[0]
    knot_count = partial.shape[0]
    load_copy = pltpu.make_async_copy(load, load_v, local_sem.at[0])
    rest_copy = pltpu.make_async_copy(rest, rest_v, local_sem.at[1])
    load_copy.start()
    stat_v[0] = stats[...]
    greet(i, n, bits)

    def near_copy(s):
        return remote(
            returned.at[far + s], near_v.at[s], near_send.at[s], near_recv.at[s], lax.rem(i + n - 1, n)
        )

    def far_copy(q):
        return remote(returned.at[q], far_v.at[q], far_send.at[q], far_recv.at[q], lax.rem(i + n - 2, n))

    @pl.when(i > 1)
    def _():
        for q in range(far):
            far_copy(q).start()

    def stat_copy(t):
        return remote(stat_v.at[t], stat_in.at[t], stat_send.at[t], stat_recv.at[t], flip(i, t))

    def piece(j):
        return pl.ds(pl.multiple_of(j * rows, rows), rows)

    def start_of(t):
        return n - (n >> t)

    def part_copy(t, j, m):
        at = start_of(t) + m
        return remote(
            partial.at[piece(j)], landed.at[at], part_send.at[at], part_recv.at[at], flip(i, t)
        )

    stat_copy(0).start()
    load_copy.wait()
    rest_copy.start()

    tile = min(256, knot_count)
    pairs = tile // rows // 2
    other = 1 - lax.rem(i, 2)

    def tile_step(u, carry):
        at = pl.multiple_of(u * tile, tile)
        partial[pl.ds(at, tile), :] = lax.dot_general(
            load_v[:, pl.ds(at, tile)], half[...], (((0,), (0,)), ((), ())), preferred_element_type=F32
        )
        for q in range(pairs):
            m = u * pairs + q
            part_copy(0, 2 * m + other, m).start()
        return carry

    lax.fori_loop(0, knot_count // tile, tile_step, 0)

    def settle(j, steps):
        for t in range(steps):
            m = j // (2 << t)
            at = start_of(t) + m
            part_copy(t, j, m).wait_recv()
            partial[piece(j), :] += landed[at]

    for t in range(1, bits + 1):
        stat_copy(t - 1).wait_recv()
        stat_v[t] = stat_v[t - 1] + stat_in[t - 1]
        if t < bits:
            stat_copy(t).start()
            low = lax.rem(flip(i, t), 2 << t)
            for m in range(n >> (t + 1)):
                j = low + m * (2 << t)
                settle(j, t)
                part_copy(t, j, m).start()
        if t == 2:

            @pl.when(i > 0)
            def _():
                for s in reversed(range(slots)):
                    near_copy(s).start()

    settle(i, bits)
    score[...] = partial[piece(i), :]
    totals[...] = stat_v[bits]

    rest_copy.wait()
    for s in reversed(range(slots)):

        @pl.when(i < n - 1)
        def _():
            near_copy(s).wait_recv()
            rest_v[s] = rest_v[s] - near_v[s].astype(F32)

        if s >= slots - far:

            @pl.when(i < n - 2)
            def _():
                far_copy(s - (slots - far)).wait_recv()
                rest_v[s] = rest_v[s] - far_v[s - (slots - far)].astype(F32)

    @pl.when(i > 0)
    def _():
        for s in range(slots):
            near_copy(s).wait_send()

    @pl.when(i > 1)
    def _():
        for q in range(far):
            far_copy(q).wait_send()

    for t in range(bits):
        stat_copy(t).wait_send()
        low = lax.rem(flip(i, t), 2 << t)
        for m in range(n >> (t + 1)):
            part_copy(t, low + m * (2 << t), m).wait_send()


def vmem():
    return pl.BlockSpec(memory_space=pltpu.VMEM)


def smem():
    return pl.BlockSpec(memory_space=pltpu.SMEM)


def anywhere():
    return pl.BlockSpec(memory_space=pl.ANY)


def local(n, obs, counts, neighbours, krig, knot_load, knot_values, whiten, noise_var):
    bits = n.bit_length() - 1
    slots, points, fields = obs.shape
    knot_count = knot_load.shape[2]
    neigh = neighbours.shape[1]
    far = REACH - slots
    window_length = REACH + slots
    rows = knot_values.shape[0]
    dma = pltpu.SemaphoreType.DMA

    window, base = pl.pallas_call(
        functools.partial(gather_kernel, n, bits),
        out_shape=(
            jax.ShapeDtypeStruct((window_length, points, fields), BF16),
            jax.ShapeDtypeStruct((slots, points, fields), F32),
        ),
        in_specs=[smem(), anywhere(), anywhere(), vmem()],
        out_specs=(vmem(), vmem()),
        scratch_shapes=[
            pltpu.VMEM((slots, points, fields), BF16),
            pltpu.VMEM((slots, points, knot_count), BF16),
            pltpu.VMEM((knot_count, fields), BF16),
            dma((slots,)), dma((slots,)), dma((slots,)), dma((slots,)),
            dma((far,)), dma((far,)), dma((far,)), dma((n - 1,)), dma((n - 1,)),
        ],
        compiler_params=pltpu.CompilerParams(
            collective_id=0, has_side_effects=True, vmem_limit_bytes=VMEM_LIMIT
        ),
    )(counts, obs, knot_load, knot_values)

    group = 2 - slots % 2

    def whole(*shape):
        return pl.BlockSpec(shape, lambda s, *_: (0,) * len(shape))

    def slot(*shape):
        return pl.BlockSpec((group,) + shape, lambda s, *_: (s,) + (0,) * len(shape))

    returned, adjoint_half, rest, stats = pl.pallas_call(
        block_kernel,
        out_shape=(
            jax.ShapeDtypeStruct((REACH, points, fields), BF16),
            jax.ShapeDtypeStruct((slots, points, fields), BF16),
            jax.ShapeDtypeStruct((slots, points, fields), F32),
            jax.ShapeDtypeStruct((8, fields), F32),
        ),
        grid_spec=pltpu.PrefetchScalarGridSpec(
            num_scalar_prefetch=2,
            grid=(slots // group,),
            in_specs=[
                whole(window_length, points, fields),
                slot(points, fields),
                slot(neigh, points, points),
                slot(points, points),
            ],
            out_specs=(
                whole(REACH, points, fields),
                slot(points, fields),
                whole(slots, points, fields),
                whole(8, fields),
            ),
            scratch_shapes=[
                pltpu.VMEM((window_length + 1, points, fields), F32),
                pltpu.VMEM((slots, points, fields), F32),
            ],
        ),
        compiler_params=pltpu.CompilerParams(
            dimension_semantics=("arbitrary",), vmem_limit_bytes=VMEM_LIMIT
        ),
    )(neighbours, counts, window, base, krig, whiten)

    rest, totals, score = pl.pallas_call(
        functools.partial(score_kernel, n, bits),
        out_shape=(
            jax.ShapeDtypeStruct((slots, points, fields), F32),
            jax.ShapeDtypeStruct((8, fields), F32),
            jax.ShapeDtypeStruct((rows, fields), F32),
        ),
        in_specs=[vmem(), vmem(), anywhere(), anywhere(), anywhere()],
        out_specs=(vmem(), vmem(), vmem()),
        scratch_shapes=[
            pltpu.VMEM((slots * points, knot_count), BF16),
            pltpu.VMEM((slots, points, fields), BF16),
            pltpu.VMEM((far, points, fields), BF16),
            pltpu.VMEM((knot_count, fields), F32),
            pltpu.VMEM((n - 1, rows, fields), F32),
            pltpu.VMEM((bits + 1, 8, fields), F32),
            pltpu.VMEM((bits, 8, fields), F32),
            dma((2,)), dma((slots,)), dma((slots,)), dma((far,)), dma((far,)),
            dma((n - 1,)), dma((n - 1,)), dma((bits,)), dma((bits,)),
        ],
        compiler_params=pltpu.CompilerParams(
            collective_id=1, has_side_effects=True, vmem_limit_bytes=VMEM_LIMIT
        ),
    )(
        stats,
        adjoint_half.reshape(slots * points, fields),
        returned,
        rest,
        knot_load.reshape(slots * points, knot_count),
    )
    valid = jnp.arange(points)[None, :, None] < counts[:, None, None]
    precision = jnp.where(valid, rest, 0.0)
    masked = jnp.where(valid, obs.astype(F32), 0.0)
    posterior = (masked - noise_var[None, None, :] * precision).astype(BF16)
    loglik = (totals[1] - 0.5 * totals[0]) / totals[2]
    return posterior, loglik, score


def solution(mesh):
    in_specs = (
        P(("parts", "space"), None, None),
        P(("parts", "space")),
        P(("parts", "space"), None),
        P(("parts", "space"), None, None, None),
        P(("parts", "space"), None, None),
        P(("parts", "space"), None),
        P(("parts", "space"), None, None),
        P(),
    )
    out_specs = (P(("parts", "space"), None, None), P("parts"), P(("parts", "space"), None))
    return jax.shard_map(
        functools.partial(local, mesh.shape["space"]),
        mesh=mesh,
        in_specs=in_specs,
        out_specs=out_specs,
        check_vma=False,
    )
```

```python
import functools

import jax
import jax.numpy as jnp
from jax import lax
from jax.experimental import pallas as pl
from jax.experimental.pallas import tpu as pltpu
from jax.sharding import PartitionSpec as P

REACH = 9
VMEM_LIMIT = 56 * 1024 * 1024
F32 = jnp.float32
BF16 = jnp.bfloat16


def remote(src, dst, send_sem, recv_sem, target):
    return pltpu.make_async_remote_copy(
        src_ref=src,
        dst_ref=dst,
        send_sem=send_sem,
        recv_sem=recv_sem,
        device_id={"space": target},
        device_id_type=pl.DeviceIdType.MESH,
    )


def flip(i, bit):
    size = 1 << bit
    return i + size - 2 * size * ((i // size) % 2)


def greet(i, n, bits):
    barrier = pltpu.get_barrier_semaphore()
    others = [flip(i, bit) for bit in range(bits)]
    others += [lax.rem(i + by, n) for by in (1, 2, n - 1, n - 2)]
    for other in others:
        pl.semaphore_signal(
            barrier, inc=1, device_id={"space": other}, device_id_type=pl.DeviceIdType.MESH
        )
    pl.semaphore_wait(barrier, len(others))


def row_mask(points, count):
    return (lax.broadcasted_iota(jnp.int32, (points, 1), 0) < count).astype(F32)


def gather_kernel(
    n, bits, counts, obs, load, values, window, base, obs_v, load_v, knots,
    obs_sem, load_sem, near_send, near_recv, far_send, far_recv, pass_send, knot_send, knot_recv,
):
    i = lax.axis_index("space")
    slots, points, fields = obs_v.shape
    far = REACH - slots
    rows = values.shape[0]
    obs_copies = [pltpu.make_async_copy(obs.at[s], obs_v.at[s], obs_sem.at[s]) for s in range(slots)]
    load_copies = [pltpu.make_async_copy(load.at[s], load_v.at[s], load_sem.at[s]) for s in range(slots)]
    for s in reversed(range(slots)):
        obs_copies[s].start()
    for s in range(slots):
        load_copies[s].start()

    def chunk(j):
        return knots.at[pl.ds(pl.multiple_of(j * rows, rows), rows)]

    knots[pl.ds(pl.multiple_of(i * rows, rows), rows), :] = values[...]
    greet(i, n, bits)

    def exchange(first, count, stride, mine, partner, theirs):
        sends, receives = [], []
        for m in range(count):
            at = first + m
            out, back = chunk(mine + m * stride), chunk(theirs + m * stride)
            sends.append(remote(out, out, knot_send.at[at], knot_recv.at[at], partner))
            receives.append(remote(back, back, knot_send.at[at], knot_recv.at[at], partner))
        return sends, receives

    def line_step(t):
        bit = bits - 1 - t
        stride = 2 << bit
        partner = flip(i, bit)
        return exchange(
            (1 << t) - 1, n // stride, stride, lax.rem(i, stride), partner, lax.rem(partner, stride)
        )

    def start(copies):
        for copy in copies:
            copy.start()

    lines = bits - 2
    held = n // 4
    steps = [line_step(t) for t in range(lines)]
    pair, side = flip(i, 0), flip(i, 1)
    mine, pair_low, side_low = lax.rem(i, 4), lax.rem(pair, 4), lax.rem(side, 4)
    over_pair = exchange(held - 1, held, 4, mine, pair, pair_low)
    over_side = exchange(2 * held - 1, held, 4, mine, side, side_low)
    relay = exchange(3 * held - 1, held, 4, side_low, pair, flip(side_low, 0))
    start(steps[0][0])

    def near_copy(s, to):
        return remote(window.at[REACH + s], window.at[far + s], near_send.at[s], near_recv.at[s], to)

    def far_copy(q, to):
        return remote(window.at[REACH + slots - far + q], window.at[q], far_send.at[q], far_recv.at[q], to)

    def pass_copy(q, to):
        return remote(window.at[REACH - far + q], window.at[q], pass_send.at[q], far_recv.at[q], to)

    even = lax.rem(i, 2) == 0
    has_next = i < n - 1
    sends_far = jnp.logical_and(even, i < n - 2)
    passes = jnp.logical_and(even, i > 0)
    next_one, next_two = lax.rem(i + 1, n), lax.rem(i + 2, n)

    for s in reversed(range(slots)):
        obs_copies[s].wait()
        window[REACH + s] = (obs_v[s].astype(F32) * row_mask(points, counts[s])).astype(BF16)

        @pl.when(has_next)
        def _():
            near_copy(s, next_one).start()

        if s >= slots - far:

            @pl.when(sends_far)
            def _():
                far_copy(s - (slots - far), next_two).start()

    for t in range(lines):
        for copy in steps[t][1]:
            copy.wait_recv()
        start(steps[t + 1][0] if t + 1 < lines else over_side[0] + over_pair[0])

    width = 2 * rows
    staged = width % 128 == 0

    def coarse_part(s, low):
        total = None
        for m in range(held):
            at = pl.ds(pl.multiple_of((low + 4 * m) * rows, width), width)
            term = jnp.dot(load_v[s, :, at], knots[at, :], preferred_element_type=F32)
            total = term if total is None else total + term
        return total

    for s in range(slots):
        load_copies[s].wait()
    for copy in over_pair[1]:
        copy.wait_recv()
    if staged:

        def first_step(s, carry):
            base[s] = window[REACH + s].astype(F32) - coarse_part(s, mine - lax.rem(mine, 2))
            return carry

        lax.fori_loop(0, slots, first_step, 0)

    for arrive, onward in zip(over_side[1], relay[0]):
        arrive.wait_recv()
        onward.start()

    for q in reversed(range(far)):

        @pl.when(i > 0)
        def _():
            near_copy(slots - far + q, next_one).wait_recv()

        @pl.when(passes)
        def _():
            pass_copy(q, next_one).start()

    for copy in relay[1]:
        copy.wait_recv()

    def last_step(s, carry):
        if staged:
            base[s] -= coarse_part(s, side_low - lax.rem(side_low, 2))
        else:
            coarse = jnp.dot(load_v[s], knots[...], preferred_element_type=F32)
            base[s] = window[REACH + s].astype(F32) - coarse
        return carry

    lax.fori_loop(0, slots, last_step, 0)

    @pl.when(i > 0)
    def _():
        for s in range(slots - far):
            near_copy(s, next_one).wait_recv()

    @pl.when(i > 1)
    def _():
        for q in range(far):
            far_copy(q, next_two).wait_recv()

    @pl.when(has_next)
    def _():
        for s in range(slots):
            near_copy(s, next_one).wait_send()

    @pl.when(sends_far)
    def _():
        for q in range(far):
            far_copy(q, next_two).wait_send()

    @pl.when(passes)
    def _():
        for q in range(far):
            pass_copy(q, next_one).wait_send()

    for sends, _ in steps + [over_pair, over_side, relay]:
        for copy in sends:
            copy.wait_send()


def block_kernel(
    near, counts, window, base, krig, whiten, returned, adjoint_half, rest, stats, sums, adjoints
):
    step = pl.program_id(0)
    group, neigh, points = krig.shape[0], krig.shape[1], krig.shape[2]
    window_length = window.shape[0]
    slots = window_length - REACH
    anchor = lax.axis_index("space") * slots - REACH
    members = range(group)
    ids = [step * group + g for g in members]
    masks = [row_mask(points, counts[s]) for s in ids]

    @pl.when(step == 0)
    def _():
        sums[...] = jnp.zeros_like(sums)
        stats[...] = jnp.zeros_like(stats)

    places = [[near[s, k] - anchor for k in range(neigh)] for s in ids]
    valid = [[near[s, k] >= 0 for k in range(neigh)] for s in ids]
    predicted = []
    for g in members:
        total = None
        for k in range(neigh):
            block = jnp.where(valid[g][k], krig[g, k], jnp.zeros((), BF16))
            rows = window[jnp.where(valid[g][k], places[g][k], REACH)]
            term = jnp.dot(block, rows, preferred_element_type=F32)
            total = term if total is None else total + term
        predicted.append(total)
    residual = [(masks[g] * (base[g] - predicted[g])).astype(BF16) for g in members]
    whitened = [
        masks[g] * jnp.dot(whiten[g], residual[g], preferred_element_type=F32) for g in members
    ]
    whitened_half = [w.astype(BF16) for w in whitened]
    adjoint = [
        masks[g]
        * lax.dot_general(
            whiten[g], whitened_half[g], (((0,), (0,)), ((), ())), preferred_element_type=F32
        )
        for g in members
    ]
    half = [a.astype(BF16) for a in adjoint]
    for g in members:
        adjoint_half[g] = half[g]
        adjoints[ids[g]] = adjoint[g]
    for g in members:
        for k in range(neigh):
            to = jnp.where(valid[g][k], places[g][k], window_length)
            sums[to] += lax.dot_general(
                krig[g, k], half[g], (((0,), (0,)), ((), ())), preferred_element_type=F32
            )
    diagonal_at = lax.broadcasted_iota(jnp.int32, (points, points), 0) == lax.broadcasted_iota(
        jnp.int32, (points, points), 1
    )
    for g in members:
        diagonal = jnp.sum(
            jnp.where(diagonal_at, whiten[g].astype(F32), 0.0), axis=1, keepdims=True
        )
        stats[0:1] += jnp.sum(whitened[g] * whitened[g], axis=0, keepdims=True)
        stats[1:2] += jnp.sum(masks[g] * jnp.log(diagonal), axis=0, keepdims=True)
        stats[2:3] += jnp.full((1, stats.shape[1]), counts[ids[g]].astype(F32))

    @pl.when(step == pl.num_programs(0) - 1)
    def _():
        def emit(c, carry):
            returned[c] = sums[c].astype(BF16)
            return carry

        def keep(c, carry):
            rest[c] = adjoints[c] - sums[REACH + c].astype(BF16).astype(F32)
            return carry

        lax.fori_loop(0, REACH, emit, 0)
        lax.fori_loop(0, slots, keep, 0)


def score_kernel(
    n, bits, stats, half, returned, rest, load,
    rest_v, totals, score,
    load_v, near_v, far_v, partial, landed, stat_v, stat_in,
    local_sem, near_send, near_recv, far_send, far_recv, part_send, part_recv, stat_send, stat_recv,
):
    i = lax.axis_index("space")
    slots, points, fields = rest_v.shape
    far = REACH - slots
    rows = score.shape[0]
    knot_count = partial.shape[0]
    load_copy = pltpu.make_async_copy(load, load_v, local_sem.at[0])
    rest_copy = pltpu.make_async_copy(rest, rest_v, local_sem.at[1])
    load_copy.start()
    stat_v[0] = stats[...]
    greet(i, n, bits)

    def near_copy(s):
        return remote(
            returned.at[far + s], near_v.at[s], near_send.at[s], near_recv.at[s], lax.rem(i + n - 1, n)
        )

    def far_copy(q):
        return remote(returned.at[q], far_v.at[q], far_send.at[q], far_recv.at[q], lax.rem(i + n - 2, n))

    @pl.when(i > 1)
    def _():
        for q in range(far):
            far_copy(q).start()

    def stat_copy(t):
        return remote(stat_v.at[t], stat_in.at[t], stat_send.at[t], stat_recv.at[t], flip(i, t))

    def piece(j):
        return pl.ds(pl.multiple_of(j * rows, rows), rows)

    def start_of(t):
        return n - (n >> t)

    mine = [lax.rem(i // (1 << b), 2) for b in range(bits)]
    cut = fields - max(fields // 4, 128)
    columns = [pl.ds(0, cut), pl.ds(cut, fields - cut)]
    orders = [list(range(bits)), [0] + list(range(2, bits)) + [1]]
    halves = range(len(orders))

    def number(values, places):
        total = 0
        for k, b in enumerate(places):
            total = total + values[b] * (1 << k)
        return total

    def place(h, t, values):
        return start_of(t) + number(values, sorted(orders[h][t + 1 :]))

    def part_copy(h, t, j, at):
        return remote(
            partial.at[piece(j), columns[h]],
            landed.at[at, :, columns[h]],
            part_send.at[h, at],
            part_recv.at[h, at],
            flip(i, orders[h][t]),
        )

    def sent(h, t):
        free = sorted(orders[h][t + 1 :])
        for m in range(1 << len(free)):
            values = list(mine)
            values[orders[h][t]] = 1 - mine[orders[h][t]]
            for k, b in enumerate(free):
                values[b] = (m >> k) % 2
            yield values

    stat_copy(0).start()
    load_copy.wait()
    rest_copy.start()

    tile = min(256, knot_count)
    pairs = tile // rows // 2
    other = 1 - lax.rem(i, 2)

    def tile_step(u, carry):
        at = pl.multiple_of(u * tile, tile)
        partial[pl.ds(at, tile), :] = lax.dot_general(
            load_v[:, pl.ds(at, tile)], half[...], (((0,), (0,)), ((), ())), preferred_element_type=F32
        )
        for q in range(pairs):
            m = u * pairs + q
            for h in halves:
                part_copy(h, 0, 2 * m + other, m).start()
        return carry

    lax.fori_loop(0, knot_count // tile, tile_step, 0)

    def settle(h, values, steps):
        j = number(values, range(bits))
        for t in range(steps):
            at = place(h, t, values)
            part_copy(h, t, j, at).wait_recv()
            partial[piece(j), columns[h]] += landed[at, :, columns[h]]
        return j

    for t in range(1, bits + 1):
        stat_copy(t - 1).wait_recv()
        stat_v[t] = stat_v[t - 1] + stat_in[t - 1]
        if t < bits:
            stat_copy(t).start()
            for h in halves:
                for values in sent(h, t):
                    j = settle(h, values, t)
                    part_copy(h, t, j, place(h, t, values)).start()
        if t == 1:

            @pl.when(lax.rem(i, 2) == 1)
            def _():
                for s in reversed(range(slots)):
                    near_copy(s).start()

        if t == 2:

            @pl.when(jnp.logical_and(i > 0, lax.rem(i, 2) == 0))
            def _():
                for s in reversed(range(slots)):
                    near_copy(s).start()

    for h in halves:
        settle(h, mine, bits)
    score[...] = partial[piece(i), :]
    totals[...] = stat_v[bits]

    rest_copy.wait()
    for s in reversed(range(slots)):

        @pl.when(i < n - 1)
        def _():
            near_copy(s).wait_recv()
            rest_v[s] = rest_v[s] - near_v[s].astype(F32)

        if s >= slots - far:

            @pl.when(i < n - 2)
            def _():
                far_copy(s - (slots - far)).wait_recv()
                rest_v[s] = rest_v[s] - far_v[s - (slots - far)].astype(F32)

    @pl.when(i > 0)
    def _():
        for s in range(slots):
            near_copy(s).wait_send()

    @pl.when(i > 1)
    def _():
        for q in range(far):
            far_copy(q).wait_send()

    for t in range(bits):
        stat_copy(t).wait_send()
        for h in halves:
            for values in sent(h, t):
                part_copy(h, t, number(values, range(bits)), place(h, t, values)).wait_send()


def vmem():
    return pl.BlockSpec(memory_space=pltpu.VMEM)


def smem():
    return pl.BlockSpec(memory_space=pltpu.SMEM)


def anywhere():
    return pl.BlockSpec(memory_space=pl.ANY)


def local(n, obs, counts, neighbours, krig, knot_load, knot_values, whiten, noise_var):
    bits = n.bit_length() - 1
    slots, points, fields = obs.shape
    knot_count = knot_load.shape[2]
    neigh = neighbours.shape[1]
    far = REACH - slots
    window_length = REACH + slots
    rows = knot_values.shape[0]
    dma = pltpu.SemaphoreType.DMA

    window, base = pl.pallas_call(
        functools.partial(gather_kernel, n, bits),
        out_shape=(
            jax.ShapeDtypeStruct((window_length, points, fields), BF16),
            jax.ShapeDtypeStruct((slots, points, fields), F32),
        ),
        in_specs=[smem(), anywhere(), anywhere(), vmem()],
        out_specs=(vmem(), vmem()),
        scratch_shapes=[
            pltpu.VMEM((slots, points, fields), BF16),
            pltpu.VMEM((slots, points, knot_count), BF16),
            pltpu.VMEM((knot_count, fields), BF16),
            dma((slots,)), dma((slots,)), dma((slots,)), dma((slots,)),
            dma((far,)), dma((far,)), dma((far,)), dma((n - 1,)), dma((n - 1,)),
        ],
        compiler_params=pltpu.CompilerParams(
            collective_id=0, has_side_effects=True, vmem_limit_bytes=VMEM_LIMIT
        ),
    )(counts, obs, knot_load, knot_values)

    group = 2 - slots % 2

    def whole(*shape):
        return pl.BlockSpec(shape, lambda s, *_: (0,) * len(shape))

    def slot(*shape):
        return pl.BlockSpec((group,) + shape, lambda s, *_: (s,) + (0,) * len(shape))

    returned, adjoint_half, rest, stats = pl.pallas_call(
        block_kernel,
        out_shape=(
            jax.ShapeDtypeStruct((REACH, points, fields), BF16),
            jax.ShapeDtypeStruct((slots, points, fields), BF16),
            jax.ShapeDtypeStruct((slots, points, fields), F32),
            jax.ShapeDtypeStruct((8, fields), F32),
        ),
        grid_spec=pltpu.PrefetchScalarGridSpec(
            num_scalar_prefetch=2,
            grid=(slots // group,),
            in_specs=[
                whole(window_length, points, fields),
                slot(points, fields),
                slot(neigh, points, points),
                slot(points, points),
            ],
            out_specs=(
                whole(REACH, points, fields),
                slot(points, fields),
                whole(slots, points, fields),
                whole(8, fields),
            ),
            scratch_shapes=[
                pltpu.VMEM((window_length + 1, points, fields), F32),
                pltpu.VMEM((slots, points, fields), F32),
            ],
        ),
        compiler_params=pltpu.CompilerParams(
            dimension_semantics=("arbitrary",), vmem_limit_bytes=VMEM_LIMIT
        ),
    )(neighbours, counts, window, base, krig, whiten)

    rest, totals, score = pl.pallas_call(
        functools.partial(score_kernel, n, bits),
        out_shape=(
            jax.ShapeDtypeStruct((slots, points, fields), F32),
            jax.ShapeDtypeStruct((8, fields), F32),
            jax.ShapeDtypeStruct((rows, fields), F32),
        ),
        in_specs=[vmem(), vmem(), anywhere(), anywhere(), anywhere()],
        out_specs=(vmem(), vmem(), vmem()),
        scratch_shapes=[
            pltpu.VMEM((slots * points, knot_count), BF16),
            pltpu.VMEM((slots, points, fields), BF16),
            pltpu.VMEM((far, points, fields), BF16),
            pltpu.VMEM((knot_count, fields), F32),
            pltpu.VMEM((n - 1, rows, fields), F32),
            pltpu.VMEM((bits + 1, 8, fields), F32),
            pltpu.VMEM((bits, 8, fields), F32),
            dma((2,)), dma((slots,)), dma((slots,)), dma((far,)), dma((far,)),
            dma((2, n - 1)), dma((2, n - 1)), dma((bits,)), dma((bits,)),
        ],
        compiler_params=pltpu.CompilerParams(
            collective_id=1, has_side_effects=True, vmem_limit_bytes=VMEM_LIMIT
        ),
    )(
        stats,
        adjoint_half.reshape(slots * points, fields),
        returned,
        rest,
        knot_load.reshape(slots * points, knot_count),
    )
    valid = jnp.arange(points)[None, :, None] < counts[:, None, None]
    precision = jnp.where(valid, rest, 0.0)
    masked = jnp.where(valid, obs.astype(F32), 0.0)
    posterior = (masked - noise_var[None, None, :] * precision).astype(BF16)
    loglik = (totals[1] - 0.5 * totals[0]) / totals[2]
    return posterior, loglik, score


def solution(mesh):
    in_specs = (
        P(("parts", "space"), None, None),
        P(("parts", "space")),
        P(("parts", "space"), None),
        P(("parts", "space"), None, None, None),
        P(("parts", "space"), None, None),
        P(("parts", "space"), None),
        P(("parts", "space"), None, None),
        P(),
    )
    out_specs = (P(("parts", "space"), None, None), P("parts"), P(("parts", "space"), None))
    return jax.shard_map(
        functools.partial(local, mesh.shape["space"]),
        mesh=mesh,
        in_specs=in_specs,
        out_specs=out_specs,
        check_vma=False,
    )
```
